512 devices in a mesh: expert: 32 (over x, z), row: 16 (over y, core).
Axes of the slice: x: 4, y: 8, z: 8, core: 2. Of those that a mesh axis runs over, the one named last changes fastest.
Arguments:
- momentum: bfloat16 [32, 3584, 2048], P('expert', 'row'), may hold values from -6 to 6
- gradient: bfloat16 [32, 3584, 2048], P('expert', 'row'), may hold values from -96 to 96
- basis: float32 [32, 2048, 512], P('expert', 'row'), may hold values from -0.125 to 0.125
- ranks: int32 [32], replicated, may hold values from 128 to 512, as said below
- assignment: int32 [32], replicated, may hold values from 0 to 31, each once
Outputs:
- new_momentum: bfloat16 [32, 3584, 2048], P('expert', 'row')
- update: bfloat16 [32, 3584, 2048], P('expert', 'row')
- new_basis: float32 [32, 2048, 512], P('expert', 'row')
The draws below stay inside these ranges and needn't reach their ends.
Inputs may be any that keep to these rules, and one draw needn't show every extreme that they name: `ranks`: some expert has rank 512 in every draw.
All inputs are finite; a program needn't handle non-finite values.
Results may differ from the reference program's by a relative error of at most 0.033.
Values may be sent and summed in bfloat16 or wider, within the bound.
A program may use at most 64 MiB of HBM per device.

```python
import math
import jax
import jax.numpy as jnp
from jax import lax

ROWS = 3584
FF = 2048
RANK_MAX = 512
EXPERTS = 32


def draw_ranks(key, part):
    subkeys = jax.random.split(jax.random.fold_in(key, 11), 3)
    quarter = RANK_MAX // 4
    step_size = max(RANK_MAX // 16, 1)
    base_rank = quarter + step_size * jax.random.randint(subkeys[0], (EXPERTS,), 0, 4)
    heavy_rank = jax.random.randint(subkeys[1], (EXPERTS,), RANK_MAX // 2 + RANK_MAX // 4, RANK_MAX + 1)
    order_ids = jax.random.permutation(subkeys[2], EXPERTS)
    heavy_count = max(EXPERTS // 8, 1)
    rank_vals = jnp.where(order_ids < heavy_count, heavy_rank, base_rank)
    return jnp.where(order_ids == 0, RANK_MAX, rank_vals).astype(jnp.int32)


def draw_gradient(key, part):
    subkeys = jax.random.split(jax.random.fold_in(key, 23), 3)
    expert_pos = jnp.arange(EXPERTS, dtype=jnp.float32)
    expert_scale = 1.0 + 2.0 * expert_pos / max(EXPERTS - 1, 1)
    row_pos = jnp.arange(ROWS, dtype=jnp.float32)
    row_rise = 1.0 + 2.0 * row_pos / max(ROWS - 1, 1)
    block_ids = jnp.arange(ROWS, dtype=jnp.int32) * 16 // ROWS
    block_level = jnp.exp(jax.random.uniform(subkeys[2], (EXPERTS, 16), jnp.float32, -0.5, 0.5))
    row_level = row_rise[None, :] * block_level[:, block_ids]
    values = jnp.clip(jax.random.normal(subkeys[0], (EXPERTS, ROWS, FF), jnp.float32), -3.0, 3.0)
    values = values * row_level[:, :, None]
    return (values * expert_scale[:, None, None]).astype(jnp.bfloat16)


def block_scale(stream_key, shape, cuts, low, largest):
    gain = 1.0
    for position, blocks in cuts:
        heights = jax.random.uniform(jax.random.fold_in(jax.random.fold_in(stream_key, 6), position), (blocks,), jnp.float32, low / len(cuts), largest / len(cuts))
        gain = gain * jnp.repeat(jnp.exp(heights), shape[position] // blocks).reshape((-1,) + (1,) * (len(shape) - 1 - position))
    return gain


def noise(stream_key, extent, scale, bound, cuts=(), kind=jnp.bfloat16):
    gain = block_scale(stream_key, extent, cuts, -0.22, 0.18) if cuts else 1.0
    values = jax.random.normal(stream_key, extent, jnp.float32) * scale * gain
    return jnp.minimum(jnp.maximum(values, -bound), bound).astype(kind)


def setup_inputs(seed: int = 0) -> dict:
    seeds = jax.random.split(jax.random.key(seed), 6)
    return {
        "momentum": noise(seeds[0], (EXPERTS, ROWS, FF), 1.0, 6.0, ((0, 32), (1, 16))),
        "gradient": draw_gradient(jax.random.fold_in(seeds[5], 71), 0),
        "basis": noise(seeds[2], (EXPERTS, FF, RANK_MAX), FF ** -0.5, 0.125, ((0, 32), (1, 16)), jnp.float32),
        "ranks": draw_ranks(jax.random.fold_in(seeds[5], 71), 0),
        "assignment": jax.random.permutation(seeds[4], EXPERTS).astype(jnp.int32),
    }


epsilon = 1e-06
mu_decay = 0.9
clip_target = 0.5

def one_expert(items, clip_scale):
    mom_block, grad_block, basis_block, rank_now = items
    buffer_full = mom_block.astype(jnp.float32) + clip_scale * grad_block.astype(jnp.float32)
    buffer = buffer_full.astype(jnp.bfloat16)
    keep_mask = (jnp.arange(RANK_MAX, dtype=jnp.int32) < rank_now).astype(jnp.float32)
    basis_half = (basis_block * keep_mask[None, :]).astype(jnp.bfloat16)
    power_cols = jnp.dot(buffer.astype(jnp.float32), basis_half.astype(jnp.float32), preferred_element_type=jnp.float32)
    gram_sum = lax.dot_general(power_cols.astype(jnp.float32), power_cols.astype(jnp.float32), (((0,), (0,)), ((), ())), precision=lax.Precision.HIGHEST, preferred_element_type=jnp.float32)
    gram_sum = gram_sum * keep_mask[:, None] * keep_mask[None, :] + jnp.diag(1.0 - keep_mask)
    lower_factor = jnp.linalg.cholesky(gram_sum)
    identity = jnp.eye(RANK_MAX, dtype=jnp.float32)
    inverse = lax.linalg.triangular_solve(lower_factor, identity, left_side=True, lower=True)
    orthonormal = lax.dot_general(power_cols.astype(jnp.float32), inverse.astype(jnp.float32), (((1,), (1,)), ((), ())), precision=lax.Precision.HIGHEST, preferred_element_type=jnp.float32)
    ortho_half = orthonormal.astype(jnp.bfloat16)
    factor = lax.dot_general(buffer.astype(jnp.float32), ortho_half.astype(jnp.float32), (((0,), (0,)), ((), ())), preferred_element_type=jnp.float32)
    col_sq = lax.optimization_barrier(jnp.sum(factor * factor, axis=0))
    inv_norm = lax.rsqrt(col_sq + epsilon)
    new_basis = factor * inv_norm[None, :]
    factor_half = factor.astype(jnp.bfloat16)
    feedback = lax.dot_general(ortho_half.astype(jnp.float32), factor_half.astype(jnp.float32), (((1,), (1,)), ((), ())), preferred_element_type=jnp.float32)
    new_momentum = (buffer_full - (1.0 - mu_decay) * feedback).astype(jnp.bfloat16)
    update_gain = math.sqrt(ROWS * FF / RANK_MAX)
    scaled = (orthonormal * (inv_norm * update_gain)[None, :]).astype(jnp.bfloat16)
    update = lax.dot_general(scaled.astype(jnp.float32), factor_half.astype(jnp.float32), (((1,), (1,)), ((), ())), preferred_element_type=jnp.float32).astype(jnp.bfloat16)
    return (new_momentum, update, new_basis)

def reference(momentum, gradient, basis, ranks, assignment):
    sq_sums = lax.map(lambda block: jnp.sum(jnp.square(block.astype(jnp.float32))), gradient)
    mean_sq = jnp.sum(sq_sums) / (EXPERTS * ROWS * FF)
    clip_scale = jnp.minimum(1.0, clip_target * lax.rsqrt(mean_sq + epsilon))
    rank_groups = ranks[assignment]
    return lax.map(lambda items: one_expert(items, clip_scale), (momentum, gradient, basis, rank_groups))
```

```python
import math

import jax
import jax.numpy as jnp
from jax import lax
from jax.experimental import pallas as pl
from jax.experimental.pallas import tpu as pltpu
from jax.sharding import Mesh
from jax.sharding import PartitionSpec as P

ROWS = 3584
FF = 2048
RANK = 512
X, Z, Y, C = "expert_0", "expert_1", "row_0", "row_1"
ROW = (Y, C)
EXPERT = (X, Z)
NX, NZ, NY, NC = 4, 8, 8, 2
MINE = ROWS // (NY * NC)
SLAB = FF // (NY * NC)
TILE = 128
TILES = RANK // TILE
PAIRS = [(i, j) for i in range(TILES) for j in range(i, TILES)]
PACKED = len(PAIRS) * TILE
HALF = PACKED // NC
PIECE = HALF // NY

EPS = 1e-06
MU_DECAY = 0.9
CLIP_TARGET = 0.5
GAIN = math.sqrt(ROWS * FF / RANK)

F32 = jnp.float32
BF16 = jnp.bfloat16
HIGHEST = lax.Precision.HIGHEST
MESH = pl.DeviceIdType.MESH


def dot(a, b, ca=1, cb=0, precision=None):
    return lax.dot_general(
        a, b, (((ca,), (cb,)), ((), ())), precision=precision, preferred_element_type=F32
    )


def split(value):
    high = value.astype(BF16)
    return high, (value - high.astype(F32)).astype(BF16)


def send(src, dst, send_sem, recv_sem, **device):
    return pltpu.make_async_remote_copy(
        src_ref=src,
        dst_ref=dst,
        send_sem=send_sem,
        recv_sem=recv_sem,
        device_id=device,
        device_id_type=MESH,
    )


def tile_inverse(z, hook):
    lane = lax.broadcasted_iota(jnp.int32, (1, TILE), 1)
    sub = lax.broadcasted_iota(jnp.int32, (8, 1), 0)
    full = (8, TILE)
    done = []
    for s in range(TILE // 8):
        lo = 8 * s
        rest = TILE - lo - 8
        top = z[:8]
        cols = [jnp.broadcast_to(top[:, lo + k : lo + k + 1], full) for k in range(8)]
        a = {
            (i, k): jnp.broadcast_to(cols[k][i : i + 1, :], full)
            for k in range(8)
            for i in range(k + 1)
        }
        inside = (lane >= lo) & (lane < lo + 8)
        rows = []
        for i in range(8):
            row = jnp.where(inside, (lane == lo + i).astype(F32), top[i : i + 1, :])
            rows.append(jnp.broadcast_to(row, full))
        u = {}
        rec = []
        for j in range(8):
            rec.append(1.0 / a[j, j])
            for i in range(j + 1, 8):
                u[j, i] = a[j, i] * rec[j]
            for i in range(j + 1, 8):
                for k in range(i, 8):
                    a[i, k] = a[i, k] - u[j, i] * a[j, k]
            for i in range(j + 1, 8):
                rows[i] = rows[i] - u[j, i] * rows[j]
        out = rows[0] * lax.rsqrt(a[0, 0])
        for j in range(1, 8):
            out = jnp.where(sub == j, rows[j] * lax.rsqrt(a[j, j]), out)
        done.append(jnp.where(lane < lo + 8, out, 0.0))
        if rest:
            below = z[8:]
            scaled = [rows[j] * rec[j] for j in range(8)]
            new = []
            for g in range(rest // 8):
                zg = below[8 * g : 8 * g + 8]
                c = [jnp.broadcast_to(zg[:, lo + k : lo + k + 1], full) for k in range(8)]
                for j in range(8):
                    for i in range(j + 1, 8):
                        c[i] = c[i] - c[j] * u[j, i]
                acc = jnp.where(inside, 0.0, zg)
                for j in range(8):
                    acc = acc - c[j] * scaled[j]
                new.append(acc)
            z = jnp.concatenate(new, axis=0) if len(new) > 1 else new[0]
        hook()
    return jnp.concatenate(done, axis=0)


class Gather:
    def __init__(self, buf, half, sems, y, c):
        self.buf, self.half, self.y, self.c = buf, half, y, c
        self.ring_send, self.ring_recv, self.core_send, self.core_recv = sems
        self.sent = []

    def part(self, chip, core, h):
        return self.buf.at[2 * lax.rem(chip, NY) + core, pl.ds(h * self.half, self.half)]

    def origin(self, side, k):
        return self.y + (NY - 1 - k if side == 0 else 1 + k)

    def hop(self, side, k, h, chip):
        ref = self.part(chip, self.c, h)
        i = side * 8 + k * 2 + h
        to = lax.rem(self.y + (1 if side == 0 else NY - 1), NY)
        return send(ref, ref, self.ring_send.at[i], self.ring_recv.at[i], row_0=to)

    def across(self, i, chip, core, h):
        ref = self.part(chip, core, h)
        return send(ref, ref, self.core_send.at[i], self.core_recv.at[i], row_1=1 - self.c)

    def begin(self):
        for h in range(2):
            for side in range(2):
                copy = self.hop(side, 0, h, self.y)
                copy.start()
                self.sent.append(copy)
        for h in range(2):
            copy = self.across(16 + h, self.y, self.c, h)
            copy.start()
            self.sent.append(copy)

    @staticmethod
    def halves(k, side):
        return (0, 1) if k < 3 else (side,)

    def steps(self):
        return [(k, h) for k in range(4) for h in range(2)]

    def step(self, k, h):
        for side in range(2):
            if h not in self.halves(k, side):
                continue
            chip = self.origin(side, k)
            self.hop(side, k, h, chip).wait_recv()
            if k < 3 and h in self.halves(k + 1, side):
                copy = self.hop(side, k + 1, h, chip)
                copy.start()
                self.sent.append(copy)
            copy = self.across(side * 8 + k * 2 + h, chip, self.c, h)
            copy.start()
            self.sent.append(copy)

    def own_across(self):
        for h in range(2):
            self.across(16 + h, self.y, 1 - self.c, h).wait_recv()

    def far_across(self, k):
        for h in range(2):
            for side in range(2):
                if h in self.halves(k, side):
                    chip = self.origin(side, k)
                    self.across(side * 8 + k * 2 + h, chip, 1 - self.c, h).wait_recv()

    def drain(self):
        for copy in self.sent:
            copy.wait_send()


def kernel(
    mom_hbm,
    grad_hbm,
    basis_ref,
    ranks_ref,
    assign_ref,
    nm_hbm,
    up_hbm,
    nb_ref,
    mom,
    grad,
    full,
    buf,
    ball,
    power,
    packed,
    gtx,
    grx,
    gsum,
    gpieces,
    gall,
    tpart,
    ttx,
    trx,
    rtx,
    rrx,
    tall,
    amat,
    wmat,
    fhalf,
    nm,
    up,
    ps_tx,
    ps_rx,
    load_sem,
    out_sem,
    ps_send,
    ps_recv,
    b_ring_send,
    b_ring_recv,
    b_core_send,
    b_core_recv,
    t_ring_send,
    t_ring_recv,
    t_core_send,
    t_core_recv,
    g_send,
    g_recv,
    r_send,
    r_recv,
    x_send,
    x_recv,
):
    x, z, y, c = (lax.axis_index(a) for a in (X, Z, Y, C))
    load_grad = pltpu.make_async_copy(grad_hbm, grad, load_sem.at[0])
    load_mom = pltpu.make_async_copy(mom_hbm, mom, load_sem.at[1])
    load_grad.start()
    load_mom.start()

    peers = [{C: 1 - c}]
    peers += [{Z: lax.rem(z + k, NZ)} for k in range(1, NZ)]
    peers += [{X: lax.rem(x + k, NX)} for k in range(1, NX)]
    peers += [{Y: lax.rem(y + k, NY)} for k in range(1, NY)]
    barrier = pltpu.get_barrier_semaphore()
    for peer in peers:
        pl.semaphore_signal(barrier, inc=1, device_id=peer, device_id_type=MESH)

    rank = ranks_ref[assign_ref[x * NZ + z]]
    col_id = lax.broadcasted_iota(jnp.int32, (1, RANK), 1)
    mine = 2 * y + c
    ball[mine] = jnp.where(col_id < rank, basis_ref[...], 0.0).astype(BF16)
    pl.semaphore_wait(barrier, len(peers))

    gather_b = Gather(ball, SLAB // 2, (b_ring_send, b_ring_recv, b_core_send, b_core_recv), y, c)
    gather_b.begin()

    load_grad.wait()

    def add_squares(i, acc):
        rows = grad[pl.ds(pl.multiple_of(i * 16, 16), 16), :].astype(F32)
        acc = list(acc)
        for t in range(FF // TILE):
            for r in range(2):
                piece = rows[8 * r : 8 * r + 8, t * TILE : (t + 1) * TILE]
                acc[(2 * t + r) % 4] = acc[(2 * t + r) % 4] + piece * piece
        return tuple(acc)

    zero = jnp.zeros((8, TILE), F32)
    acc = lax.fori_loop(0, MINE // 16, add_squares, (zero,) * 4)
    total = (acc[0] + acc[1]) + (acc[2] + acc[3])
    all_sent = []

    def share(stage, base, value, axis, place, size):
        ps_tx[stage] = value
        copies = []
        for k in range(1, size):
            i = base + k - 1
            copy = send(
                ps_tx.at[stage],
                ps_rx.at[i],
                ps_send.at[i],
                ps_recv.at[i],
                **{axis: lax.rem(place + k, size)},
            )
            copy.start()
            copies.append(copy)
        all_sent.extend(copies)
        return copies

    def collect(base, value, copies):
        for k, copy in enumerate(copies):
            copy.wait_recv()
            value = value + ps_rx[base + k]
        return value

    stage_c = share(0, 0, total, C, c, NC)
    total = collect(0, total, stage_c)
    stage_z = share(1, 1, total, Z, z, NZ)
    gather_b.step(0, 0)
    total = collect(1, total, stage_z)
    stage_x = share(2, 8, total, X, x, NX)
    gather_b.step(0, 1)
    total = collect(8, total, stage_x)
    stage_y = share(3, 11, total, Y, y, NY)
    gather_b.step(1, 0)
    gather_b.step(1, 1)
    total = collect(11, total, stage_y)
    mean_sq = jnp.sum(total, keepdims=True) / float(NX * NZ * ROWS * FF)
    clip = jnp.minimum(1.0, CLIP_TARGET * lax.rsqrt(mean_sq + EPS))

    load_mom.wait()
    for i in range(MINE // 32):
        at = pl.ds(i * 32, 32)
        value = mom[at, :].astype(F32) + clip * grad[at, :].astype(F32)
        full[at, :] = value
        buf[at, :] = value.astype(BF16)
    gather_b.step(2, 0)
    gather_b.step(2, 1)

    def times_chip(chip):
        chip = lax.rem(chip, NY)
        cols = pl.ds(pl.multiple_of(chip * 2 * SLAB, 2 * SLAB), 2 * SLAB)
        basis = ball[pl.ds(2 * chip, 2)].reshape(2 * SLAB, RANK)
        return dot(buf[:, cols], basis)

    gather_b.own_across()
    power[...] = times_chip(y)
    for k in range(3):
        gather_b.far_across(k)
        power[...] = power[...] + (times_chip(y + NY - 1 - k) + times_chip(y + 1 + k))
    gather_b.step(3, 0)
    gather_b.step(3, 1)
    gather_b.far_across(3)
    pw = power[...] + times_chip(y + 4)
    power[...] = pw

    turned = pw.T
    pt_hi, pt_lo = split(turned)
    p_hi, p_lo = split(pw)
    at = 0
    for i in range(TILES):
        r = slice(i * TILE, (i + 1) * TILE)
        strip = (
            dot(pt_hi[r], p_hi[:, i * TILE :])
            + dot(pt_hi[r], p_lo[:, i * TILE :])
            + dot(pt_lo[r], p_hi[:, i * TILE :])
        )
        for j in range(TILES - i):
            packed[at : at + TILE, :] = strip[:, j * TILE : (j + 1) * TILE]
            at += TILE
    other = pl.ds(pl.multiple_of((1 - c) * HALF, HALF), HALF)
    own_half = pl.ds(pl.multiple_of(c * HALF, HALF), HALF)
    gtx[...] = packed[other, :].astype(BF16)
    g_across = send(gtx, grx, g_send.at[0], g_recv.at[0], row_1=1 - c)
    g_across.start()
    all_sent.append(g_across)

    for chip in range(NY):
        part = dot(pt_hi, buf[:, chip * 2 * SLAB : (chip + 1) * 2 * SLAB])
        tpart[0, chip] = part[:, :SLAB]
        tpart[1, chip] = part[:, SLAB:]
    for chip in range(NY):
        ttx[chip] = tpart[1 - c, chip].astype(BF16)
    t_across = send(ttx, trx, x_send.at[0], x_recv.at[0], row_1=1 - c)

    g_across.wait_recv()
    gsum[...] = packed[own_half, :] + grx[...].astype(F32)
    for k in range(NY):
        gpieces[NY + k] = gsum[pl.ds(k * PIECE, PIECE), :].astype(BF16)
    copies = []
    for k in range(1, NY):
        to = lax.rem(y + k, NY)
        copy = send(
            gpieces.at[NY + to], gpieces.at[k], g_send.at[k], g_recv.at[k], row_0=to
        )
        copy.start()
        copies.append(copy)
    t_across.start()
    all_sent.extend(copies)
    all_sent.append(t_across)
    own_piece = gsum[pl.ds(pl.multiple_of(y * PIECE, PIECE), PIECE), :]
    for k, copy in enumerate(copies):
        copy.wait_recv()
        own_piece = own_piece + gpieces[k + 1].astype(F32)
    here = pl.ds(pl.multiple_of(c * HALF + y * PIECE, PIECE), PIECE)
    gall[here, :] = own_piece.astype(BF16)
    copies = []
    for k in range(1, NY):
        copy = send(
            gall.at[here],
            gall.at[here],
            g_send.at[NY + k],
            g_recv.at[NY + k],
            row_0=lax.rem(y + k, NY),
        )
        copy.start()
        copies.append(copy)
    all_sent.extend(copies)

    quarter = RANK // 2

    def both(chip):
        chip = lax.rem(chip, NY)
        return tpart[c, chip] + trx[chip].astype(F32)

    def ring(side, i, h):
        at = pl.ds(h * quarter, quarter)
        n = side * 8 + i * 2 + h
        to = lax.rem(y + (1 if side == 0 else NY - 1), NY)
        return send(
            rtx.at[side * 4 + i, at], rrx.at[side * 4 + i, at], r_send.at[n], r_recv.at[n], row_0=to
        )

    def reduce_step(i, h):
        for side in range(2):
            if i == 0 and h != side:
                continue
            chip = lax.rem(y + (4 - i if side == 0 else NY - 4 + i), NY)
            at = pl.ds(h * quarter, quarter)
            value = tpart[c, chip, at] + trx[chip, at].astype(F32)
            if i > 1 or (i == 1 and h == side):
                ring(side, i - 1, h).wait_recv()
                value = value + rrx[side * 4 + i - 1, at].astype(F32)
            rtx[side * 4 + i, at] = value.astype(BF16)
            copy = ring(side, i, h)
            copy.start()
            all_sent.append(copy)

    gather_t = Gather(tall, quarter, (t_ring_send, t_ring_recv, t_core_send, t_core_recv), y, c)

    def reduce_first():
        t_across.wait_recv()
        reduce_step(0, 0)
        reduce_step(0, 1)

    def reduce_last():
        for h in range(2):
            at = pl.ds(h * quarter, quarter)
            value = tpart[c, y, at] + trx[y, at].astype(F32)
            for side in range(2):
                ring(side, 3, h).wait_recv()
                value = value + rrx[side * 4 + 3, at].astype(F32)
            tall[mine, at] = value.astype(BF16)
        gather_t.begin()

    def job(fn, *args):
        return lambda: fn(*args)

    jobs = [reduce_first]
    for i in range(1, 4):
        jobs += [job(reduce_step, i, h) for h in range(2)]
    jobs += [reduce_last]
    jobs += [job(gather_t.step, k, h) for k, h in gather_t.steps()]

    jobs.pop(0)()
    for copy in copies:
        copy.wait_recv()
    g_half = send(gall.at[own_half], gall.at[own_half], g_send.at[8], g_recv.at[8], row_1=1 - c)
    g_half.start()
    all_sent.append(g_half)
    send(gall.at[other], gall.at[other], g_send.at[8], g_recv.at[8], row_1=1 - c).wait_recv()

    row_id = lax.broadcasted_iota(jnp.int32, (TILE, 1), 0)
    lane_id = lax.broadcasted_iota(jnp.int32, (1, TILE), 1)
    for n, (i, j) in enumerate(PAIRS):
        r, l = row_id + i * TILE, lane_id + j * TILE
        value = gall[n * TILE : (n + 1) * TILE, :].astype(F32)
        value = jnp.where((r < rank) & (l < rank), value, 0.0)
        if i == j:
            value = value + jnp.where((r == l) & (r >= rank), 1.0, 0.0)
        amat[i * TILE : (i + 1) * TILE, j * TILE : (j + 1) * TILE] = value
    wmat[...] = jnp.zeros_like(wmat)

    ticks = [0]

    def hook():
        ticks[0] += 1
        if ticks[0] % 4 == 0 and jobs:
            jobs.pop(0)()

    for b in range(TILES):
        lo, hi = b * TILE, (b + 1) * TILE
        inv = tile_inverse(amat[lo:hi, lo:hi], hook)
        if b:
            wmat[lo:hi, :lo] = dot(inv, wmat[lo:hi, :lo], precision=HIGHEST)
        wmat[lo:hi, lo:hi] = inv
        if b < TILES - 1:
            strip = dot(inv, amat[lo:hi, hi:], precision=HIGHEST)
            amat[hi:, hi:] = amat[hi:, hi:] - dot(strip, strip, 0, 0, HIGHEST)
            wmat[hi:, :hi] = wmat[hi:, :hi] - dot(strip, wmat[lo:hi, :hi], 0, 0, HIGHEST)
    while jobs:
        jobs.pop(0)()

    w_hi, w_lo = split(wmat[...])
    pw = power[...]
    p_hi, p_lo = split(pw)
    ortho = dot(p_hi, w_hi, 1, 1) + dot(p_lo, w_hi, 1, 1) + dot(p_hi, w_lo, 1, 1)
    ortho_half = ortho.astype(BF16)
    gather_t.own_across()
    for k in range(4):
        gather_t.far_across(k)
    outs = []
    squares = jnp.zeros((RANK, TILE), F32)
    mid = RANK // 2
    wide = 2 * SLAB
    for chip in range(NY):
        cols = slice(chip * wide, (chip + 1) * wide)
        t = jnp.concatenate([tall[2 * chip], tall[2 * chip + 1]], axis=1)
        upper = dot(w_hi[:mid, :mid], t[:mid]) + dot(w_lo[:mid, :mid], t[:mid])
        lower = dot(w_hi[mid:], t) + dot(w_lo[mid:], t)
        fac = jnp.concatenate([upper, lower], axis=0)
        squares = squares + (fac[:, :TILE] * fac[:, :TILE] + fac[:, TILE:] * fac[:, TILE:])
        fh = fac.astype(BF16)
        fhalf[chip] = fh
        back = dot(ortho_half, fh)
        nm[:, cols] = (full[:, cols] - (1.0 - MU_DECAY) * back).astype(BF16)
        copy = pltpu.make_async_copy(nm.at[:, cols], nm_hbm.at[:, cols], out_sem.at[chip])
        copy.start()
        outs.append(copy)
    t = tall[mine]
    own_fac = dot(t, w_hi, 0, 1) + dot(t, w_lo, 0, 1)
    col_sq = jnp.sum(squares, axis=1, keepdims=True)
    inv_col = lax.rsqrt(col_sq + EPS)
    inv_norm = jnp.broadcast_to(inv_col, (RANK, TILE)).T[:1, :]
    nb_ref[...] = own_fac * inv_norm
    scaled = (ortho * (inv_norm * GAIN)).astype(BF16)
    for chip in range(NY):
        cols = slice(chip * wide, (chip + 1) * wide)
        up[:, cols] = dot(scaled, fhalf[chip]).astype(BF16)
        copy = pltpu.make_async_copy(up.at[:, cols], up_hbm.at[:, cols], out_sem.at[NY + chip])
        copy.start()
        outs.append(copy)
    for copy in all_sent:
        copy.wait_send()
    gather_b.drain()
    gather_t.drain()
    for copy in outs:
        copy.wait()


def local(momentum, gradient, basis, ranks, assignment):
    any_space = pl.BlockSpec(memory_space=pl.ANY)
    vmem = pl.BlockSpec(memory_space=pltpu.VMEM)
    smem = pl.BlockSpec(memory_space=pltpu.SMEM)
    dma = pltpu.SemaphoreType.DMA
    outs = pl.pallas_call(
        kernel,
        out_shape=(
            jax.ShapeDtypeStruct((MINE, FF), BF16),
            jax.ShapeDtypeStruct((MINE, FF), BF16),
            jax.ShapeDtypeStruct((SLAB, RANK), F32),
        ),
        in_specs=[any_space, any_space, vmem, smem, smem],
        out_specs=(any_space, any_space, vmem),
        scratch_shapes=[
            pltpu.VMEM((MINE, FF), BF16),
            pltpu.VMEM((MINE, FF), BF16),
            pltpu.VMEM((MINE, FF), F32),
            pltpu.VMEM((MINE, FF), BF16),
            pltpu.VMEM((16, SLAB, RANK), BF16),
            pltpu.VMEM((MINE, RANK), F32),
            pltpu.VMEM((PACKED, TILE), F32),
            pltpu.VMEM((HALF, TILE), BF16),
            pltpu.VMEM((HALF, TILE), BF16),
            pltpu.VMEM((HALF, TILE), F32),
            pltpu.VMEM((2 * NY, PIECE, TILE), BF16),
            pltpu.VMEM((PACKED, TILE), BF16),
            pltpu.VMEM((2, NY, RANK, SLAB), F32),
            pltpu.VMEM((NY, RANK, SLAB), BF16),
            pltpu.VMEM((NY, RANK, SLAB), BF16),
            pltpu.VMEM((8, RANK, SLAB), BF16),
            pltpu.VMEM((8, RANK, SLAB), BF16),
            pltpu.VMEM((16, RANK, SLAB), BF16),
            pltpu.VMEM((RANK, RANK), F32),
            pltpu.VMEM((RANK, RANK), F32),
            pltpu.VMEM((NY, RANK, 2 * SLAB), BF16),
            pltpu.VMEM((MINE, FF), BF16),
            pltpu.VMEM((MINE, FF), BF16),
            pltpu.VMEM((4, 8, TILE), F32),
            pltpu.VMEM((18, 8, TILE), F32),
            dma((2,)),
            dma((16,)),
            dma((18,)),
            dma((18,)),
            dma((16,)),
            dma((16,)),
            dma((18,)),
            dma((18,)),
            dma((16,)),
            dma((16,)),
            dma((18,)),
            dma((18,)),
            dma((16,)),
            dma((16,)),
            dma((16,)),
            dma((16,)),
            dma((1,)),
            dma((1,)),
        ],
        compiler_params=pltpu.CompilerParams(
            collective_id=0, has_side_effects=True, vmem_limit_bytes=52 << 20
        ),
        cost_estimate=pl.CostEstimate(
            flops=4 << 30, bytes_accessed=5 << 20, transcendentals=0
        ),
    )(momentum[0], gradient[0], basis[0], ranks, assignment)
    return tuple(o[None] for o in outs)


def solution(mesh):
    torus = Mesh(mesh.devices.reshape(NX, NZ, NY, NC), (X, Z, Y, C))
    return jax.shard_map(
        local,
        mesh=torus,
        in_specs=(P(EXPERT, ROW, None), P(EXPERT, ROW, None), P(EXPERT, ROW, None), P(), P()),
        out_specs=(P(EXPERT, ROW, None), P(EXPERT, ROW, None), P(EXPERT, ROW, None)),
        check_vma=False,
    )
```

```python
import math

import jax
import jax.numpy as jnp
from jax import lax
from jax.experimental import pallas as pl
from jax.experimental.pallas import tpu as pltpu
from jax.sharding import Mesh
from jax.sharding import PartitionSpec as P

ROWS = 3584
FF = 2048
RANK = 512
X, Z, Y, C = "expert_0", "expert_1", "row_0", "row_1"
ROW = (Y, C)
EXPERT = (X, Z)
NX, NZ, NY, NC = 4, 8, 8, 2
MINE = ROWS // (NY * NC)
SLAB = FF // (NY * NC)
TILE = 128
TILES = RANK // TILE
PAIRS = [(i, j) for i in range(TILES) for j in range(i, TILES)]
PACKED = len(PAIRS) * TILE
EARLY = 2 * TILE
LATE = PACKED - EARLY
PARTS = 4
ORDER = ((2, 3, 0, 1), (0, 1, 2, 3))

EPS = 1e-06
MU_DECAY = 0.9
CLIP_TARGET = 0.5
GAIN = math.sqrt(ROWS * FF / RANK)

T_PLAN = (2, 6, 19, 31, 11, 2)

F32 = jnp.float32
BF16 = jnp.bfloat16
HIGHEST = lax.Precision.HIGHEST
MESH = pl.DeviceIdType.MESH


def dot(a, b, ca=1, cb=0, precision=None):
    return lax.dot_general(
        a, b, (((ca,), (cb,)), ((), ())), precision=precision, preferred_element_type=F32
    )


def split(value):
    high = value.astype(BF16)
    return high, (value - high.astype(F32)).astype(BF16)


def send(src, dst, send_sem, recv_sem, **device):
    return pltpu.make_async_remote_copy(
        src_ref=src,
        dst_ref=dst,
        send_sem=send_sem,
        recv_sem=recv_sem,
        device_id=device,
        device_id_type=MESH,
    )


def tile_inverse(z, hook):
    lane = lax.broadcasted_iota(jnp.int32, (1, TILE), 1)
    sub = lax.broadcasted_iota(jnp.int32, (8, 1), 0)
    full = (8, TILE)
    done = []
    for s in range(TILE // 8):
        lo = 8 * s
        rest = TILE - lo - 8
        top = z[:8]
        cols = [jnp.broadcast_to(top[:, lo + k : lo + k + 1], full) for k in range(8)]
        a = {
            (i, k): jnp.broadcast_to(cols[k][i : i + 1, :], full)
            for k in range(8)
            for i in range(k + 1)
        }
        inside = (lane >= lo) & (lane < lo + 8)
        rows = []
        for i in range(8):
            row = jnp.where(inside, (lane == lo + i).astype(F32), top[i : i + 1, :])
            rows.append(jnp.broadcast_to(row, full))
        u = {}
        rec = []
        for j in range(8):
            rec.append(1.0 / a[j, j])
            for i in range(j + 1, 8):
                u[j, i] = a[j, i] * rec[j]
            for i in range(j + 1, 8):
                for k in range(i, 8):
                    a[i, k] = a[i, k] - u[j, i] * a[j, k]
            for i in range(j + 1, 8):
                rows[i] = rows[i] - u[j, i] * rows[j]
        out = rows[0] * lax.rsqrt(a[0, 0])
        for j in range(1, 8):
            out = jnp.where(sub == j, rows[j] * lax.rsqrt(a[j, j]), out)
        done.append(jnp.where(lane < lo + 8, out, 0.0))
        if rest:
            below = z[8:]
            scaled = [rows[j] * rec[j] for j in range(8)]
            new = []
            for g in range(rest // 8):
                zg = below[8 * g : 8 * g + 8]
                c = [jnp.broadcast_to(zg[:, lo + k : lo + k + 1], full) for k in range(8)]
                for j in range(8):
                    for i in range(j + 1, 8):
                        c[i] = c[i] - c[j] * u[j, i]
                acc = jnp.where(inside, 0.0, zg)
                for j in range(8):
                    acc = acc - c[j] * scaled[j]
                new.append(acc)
            z = jnp.concatenate(new, axis=0) if len(new) > 1 else new[0]
        hook()
    return jnp.concatenate(done, axis=0)


class Gather:
    def __init__(self, buf, rows, sems, y, c):
        self.buf, self.rows, self.y, self.c = buf, rows, y, c
        self.ring_send, self.ring_recv, self.core_send, self.core_recv = sems
        self.sent = []

    def part(self, chip, core, h):
        return self.buf.at[2 * lax.rem(chip, NY) + core, pl.ds(h * self.rows, self.rows)]

    def origin(self, side, k):
        return self.y + (NY - 1 - k if side == 0 else 1 + k)

    @staticmethod
    def index(side, k, h):
        return (side * 4 + k) * PARTS + h

    def hop(self, side, k, h, chip):
        ref = self.part(chip, self.c, h)
        i = self.index(side, k, h)
        to = lax.rem(self.y + (1 if side == 0 else NY - 1), NY)
        return send(ref, ref, self.ring_send.at[i], self.ring_recv.at[i], row_0=to)

    def across(self, i, chip, core, h):
        ref = self.part(chip, core, h)
        return send(ref, ref, self.core_send.at[i], self.core_recv.at[i], row_1=1 - self.c)

    def go(self, copy):
        copy.start()
        self.sent.append(copy)

    def begin(self):
        for q in range(PARTS):
            for side in range(2):
                self.go(self.hop(side, 0, ORDER[side][q], self.y))
        for h in range(PARTS):
            self.go(self.across(8 * PARTS + h, self.y, self.c, h))

    @staticmethod
    def pieces(k, side):
        return ORDER[side] if k < 3 else ORDER[side][: PARTS // 2]

    def step(self, k, q):
        for side in range(2):
            if q >= len(self.pieces(k, side)):
                continue
            h = ORDER[side][q]
            chip = self.origin(side, k)
            self.hop(side, k, h, chip).wait_recv()
            if k < 3 and h in self.pieces(k + 1, side):
                self.go(self.hop(side, k + 1, h, chip))
            self.go(self.across(self.index(side, k, h), chip, self.c, h))

    def own_across(self):
        for h in range(PARTS):
            self.across(8 * PARTS + h, self.y, 1 - self.c, h).wait_recv()

    def far_across(self, k):
        for side in range(2):
            for h in self.pieces(k, side):
                chip = self.origin(side, k)
                self.across(self.index(side, k, h), chip, 1 - self.c, h).wait_recv()

    def drain(self):
        for copy in self.sent:
            copy.wait_send()


class GramSum:
    def __init__(self, base, half, terms, bufs, sems, y, c):
        self.base, self.half, self.piece = base, half, half // NY
        self.terms, self.y, self.c = terms, y, c
        self.tx, self.rx, self.pieces, self.out = bufs
        self.send_sem, self.recv_sem = sems
        self.sent = []

    def go(self, copy):
        copy.start()
        self.sent.append(copy)
        return copy

    def rows(self, core, at=0, size=None):
        start = self.base + core * self.half + at
        size = self.half if size is None else size
        return pl.ds(pl.multiple_of(start, 16), size)

    def to_core(self):
        self.tx[...] = self.terms[self.rows(1 - self.c), :].astype(BF16)
        self.first = self.go(
            send(self.tx, self.rx, self.send_sem.at[0], self.recv_sem.at[0], row_1=1 - self.c)
        )

    def to_owner(self):
        self.first.wait_recv()
        own = self.rows(self.c)
        self.terms[own, :] = self.terms[own, :] + self.rx[...].astype(F32)
        for k in range(NY):
            at = self.rows(self.c, k * self.piece, self.piece)
            self.pieces[NY + k] = self.terms[at, :].astype(BF16)
        self.second = []
        for k in range(1, NY):
            to = lax.rem(self.y + k, NY)
            copy = send(
                self.pieces.at[NY + to],
                self.pieces.at[k],
                self.send_sem.at[k],
                self.recv_sem.at[k],
                row_0=to,
            )
            self.second.append(self.go(copy))

    def to_all(self):
        here = self.rows(self.c, self.y * self.piece, self.piece)
        value = self.terms[here, :]
        for k, copy in enumerate(self.second):
            copy.wait_recv()
            value = value + self.pieces[k + 1].astype(F32)
        self.out[here, :] = value.astype(BF16)
        ref = self.out.at[here]
        self.third = []
        for k in range(1, NY):
            to = lax.rem(self.y + k, NY)
            i = NY + k
            copy = send(ref, ref, self.send_sem.at[i], self.recv_sem.at[i], row_0=to)
            self.third.append(self.go(copy))

    def pass_on(self):
        for copy in self.third:
            copy.wait_recv()
        ref = self.out.at[self.rows(self.c)]
        self.go(send(ref, ref, self.send_sem.at[8], self.recv_sem.at[8], row_1=1 - self.c))

    def finish(self):
        ref = self.out.at[self.rows(1 - self.c)]
        send(ref, ref, self.send_sem.at[8], self.recv_sem.at[8], row_1=1 - self.c).wait_recv()

    def drain(self):
        for copy in self.sent:
            copy.wait_send()


def kernel(
    mom_hbm,
    grad_hbm,
    basis_hbm,
    ranks_hbm,
    assign_hbm,
    nm_hbm,
    up_hbm,
    nb_ref,
    mom,
    grad,
    basis,
    ranks,
    assign,
    full,
    buf,
    ball,
    power,
    packed,
    gtx_a,
    grx_a,
    gpieces_a,
    gtx_b,
    grx_b,
    gpieces_b,
    gall,
    tpart,
    ttx,
    trx,
    rtx,
    rrx,
    tall,
    amat,
    wmat,
    fhalf,
    own_fac,
    nm,
    up,
    ps_tx,
    ps_rx,
    load_sem,
    out_sem,
    ps_send,
    ps_recv,
    b_ring_send,
    b_ring_recv,
    b_core_send,
    b_core_recv,
    t_ring_send,
    t_ring_recv,
    t_core_send,
    t_core_recv,
    ga_send,
    ga_recv,
    gb_send,
    gb_recv,
    r_send,
    r_recv,
    x_send,
    x_recv,
):
    x, z, y, c = (lax.axis_index(a) for a in (X, Z, Y, C))
    load_grad = pltpu.make_async_copy(grad_hbm, grad, load_sem.at[0])
    load_mom = pltpu.make_async_copy(mom_hbm, mom, load_sem.at[1])
    load_basis = pltpu.make_async_copy(basis_hbm, basis, load_sem.at[2])
    load_ranks = pltpu.make_async_copy(ranks_hbm, ranks, load_sem.at[3])
    load_assign = pltpu.make_async_copy(assign_hbm, assign, load_sem.at[4])
    load_ranks.start()
    load_assign.start()
    load_basis.start()
    load_grad.start()
    load_mom.start()

    peers = [{C: 1 - c}]
    peers += [{Z: lax.rem(z + k, NZ)} for k in range(1, NZ)]
    peers += [{X: lax.rem(x + k, NX)} for k in range(1, NX)]
    peers += [{Y: lax.rem(y + k, NY)} for k in range(1, NY)]
    barrier = pltpu.get_barrier_semaphore()
    for peer in peers:
        pl.semaphore_signal(barrier, inc=1, device_id=peer, device_id_type=MESH)

    load_ranks.wait()
    load_assign.wait()
    rank = ranks[assign[x * NZ + z]]
    load_basis.wait()
    col_id = lax.broadcasted_iota(jnp.int32, (1, RANK), 1)
    mine = 2 * y + c
    ball[mine] = jnp.where(col_id < rank, basis[...], 0.0).astype(BF16)
    pl.semaphore_wait(barrier, len(peers))

    gather_b = Gather(ball, SLAB // PARTS, (b_ring_send, b_ring_recv, b_core_send, b_core_recv), y, c)
    gather_b.begin()

    load_grad.wait()

    def add_squares(i, acc):
        rows = grad[pl.ds(pl.multiple_of(i * 16, 16), 16), :].astype(F32)
        acc = list(acc)
        for t in range(FF // TILE):
            for r in range(2):
                piece = rows[8 * r : 8 * r + 8, t * TILE : (t + 1) * TILE]
                acc[(2 * t + r) % 4] = acc[(2 * t + r) % 4] + piece * piece
        return tuple(acc)

    zero = jnp.zeros((8, TILE), F32)
    acc = lax.fori_loop(0, MINE // 16, add_squares, (zero,) * 4)
    total = (acc[0] + acc[1]) + (acc[2] + acc[3])
    all_sent = []

    def share(stage, base, value, axis, place, size):
        ps_tx[stage] = value
        copies = []
        for k in range(1, size):
            i = base + k - 1
            copy = send(
                ps_tx.at[stage],
                ps_rx.at[i],
                ps_send.at[i],
                ps_recv.at[i],
                **{axis: lax.rem(place + k, size)},
            )
            copy.start()
            copies.append(copy)
        all_sent.extend(copies)
        return copies

    def collect(base, value, copies):
        for k, copy in enumerate(copies):
            copy.wait_recv()
            value = value + ps_rx[base + k]
        return value

    stage_c = share(0, 0, total, C, c, NC)
    total = collect(0, total, stage_c)
    stage_z = share(1, 1, total, Z, z, NZ)
    for q in range(PARTS):
        gather_b.step(0, q)
    total = collect(1, total, stage_z)
    stage_x = share(2, 8, total, X, x, NX)
    for q in range(PARTS):
        gather_b.step(1, q)
    total = collect(8, total, stage_x)
    stage_y = share(3, 11, total, Y, y, NY)
    gather_b.step(2, 0)
    gather_b.step(2, 1)
    total = collect(11, total, stage_y)
    gather_b.step(2, 2)
    gather_b.step(2, 3)
    mean_sq = jnp.sum(total, keepdims=True) / float(NX * NZ * ROWS * FF)
    clip = jnp.minimum(1.0, CLIP_TARGET * lax.rsqrt(mean_sq + EPS))

    load_mom.wait()
    for i in range(MINE // 32):
        at = pl.ds(i * 32, 32)
        value = mom[at, :].astype(F32) + clip * grad[at, :].astype(F32)
        full[at, :] = value
        buf[at, :] = value.astype(BF16)

    def times_chip(chip):
        chip = lax.rem(chip, NY)
        cols = pl.ds(pl.multiple_of(chip * 2 * SLAB, 2 * SLAB), 2 * SLAB)
        basis = ball[pl.ds(2 * chip, 2)].reshape(2 * SLAB, RANK)
        return dot(buf[:, cols], basis)

    gather_b.own_across()
    power[...] = times_chip(y)
    for k in range(3):
        gather_b.far_across(k)
        power[...] = power[...] + (times_chip(y + NY - 1 - k) + times_chip(y + 1 + k))
    gather_b.step(3, 0)
    gather_b.step(3, 1)
    gather_b.far_across(3)
    pw = power[...] + times_chip(y + 4)
    power[...] = pw

    turned = pw.T
    pt_hi, pt_lo = split(turned)
    p_hi, p_lo = split(pw)
    at = 0
    for i in range(TILES):
        r = slice(i * TILE, (i + 1) * TILE)
        strip = (
            dot(pt_hi[r], p_hi[:, i * TILE :])
            + dot(pt_hi[r], p_lo[:, i * TILE :])
            + dot(pt_lo[r], p_hi[:, i * TILE :])
        )
        for j in range(TILES - i):
            packed[at : at + TILE, :] = strip[:, j * TILE : (j + 1) * TILE]
            at += TILE
    early = GramSum(
        0, EARLY // 2, packed, (gtx_a, grx_a, gpieces_a, gall), (ga_send, ga_recv), y, c
    )
    late = GramSum(
        EARLY, LATE // 2, packed, (gtx_b, grx_b, gpieces_b, gall), (gb_send, gb_recv), y, c
    )
    early.to_core()
    late.to_core()

    t_across = send(ttx, trx, x_send.at[0], x_recv.at[0], row_1=1 - c)

    def terms(chips):
        for chip in chips:
            part = dot(pt_hi, buf[:, chip * 2 * SLAB : (chip + 1) * 2 * SLAB])
            tpart[0, chip] = part[:, :SLAB]
            tpart[1, chip] = part[:, SLAB:]

    terms(range(0, 2))
    early.to_owner()
    late.to_owner()
    terms(range(2, NY))
    for chip in range(NY):
        ttx[chip] = tpart[1 - c, chip].astype(BF16)
    t_across.start()
    all_sent.append(t_across)

    quarter = RANK // PARTS

    def both(chip, at):
        return tpart[c, chip, at] + trx[chip, at].astype(F32)

    def ring(side, i, h):
        at = pl.ds(h * quarter, quarter)
        n = (side * 4 + i) * PARTS + h
        to = lax.rem(y + (1 if side == 0 else NY - 1), NY)
        return send(
            rtx.at[side * 4 + i, at], rrx.at[side * 4 + i, at], r_send.at[n], r_recv.at[n], row_0=to
        )

    def reduce_step(i, q):
        for side in range(2):
            h = ORDER[side][q]
            chip = lax.rem(y + (4 - i if side == 0 else NY - 4 + i), NY)
            at = pl.ds(h * quarter, quarter)
            value = both(chip, at)
            if i > 1 or (i == 1 and q >= PARTS // 2):
                ring(side, i - 1, h).wait_recv()
                value = value + rrx[side * 4 + i - 1, at].astype(F32)
            rtx[side * 4 + i, at] = value.astype(BF16)
            copy = ring(side, i, h)
            copy.start()
            all_sent.append(copy)

    gather_t = Gather(tall, quarter, (t_ring_send, t_ring_recv, t_core_send, t_core_recv), y, c)

    def reduce_last():
        for h in range(PARTS):
            at = pl.ds(h * quarter, quarter)
            value = both(y, at)
            for side in range(2):
                ring(side, 3, h).wait_recv()
                value = value + rrx[side * 4 + 3, at].astype(F32)
            tall[mine, at] = value.astype(BF16)
        gather_t.begin()

    first, second = (0, 1), (2, 3)
    t_across.wait_recv()
    for q in second:
        reduce_step(0, q)
    early.to_all()
    for q in first:
        reduce_step(1, q)
    late.to_all()
    for q in second:
        reduce_step(1, q)
    early.pass_on()
    for q in first:
        reduce_step(2, q)
    early.finish()

    jobs = {}

    def plan(tick, fn, *args):
        jobs.setdefault(tick, []).append(lambda: fn(*args))

    for n, q in enumerate(second):
        plan(T_PLAN[0] + n, reduce_step, 2, q)
    for q in range(PARTS):
        plan(T_PLAN[1] + 3 * q, reduce_step, 3, q)
    plan(T_PLAN[2], reduce_last)
    for k in range(3):
        for q in range(PARTS):
            plan(T_PLAN[3] + T_PLAN[4] * k + T_PLAN[5] * q, gather_t.step, k, q)

    row_id = lax.broadcasted_iota(jnp.int32, (TILE, 1), 0)
    lane_id = lax.broadcasted_iota(jnp.int32, (1, TILE), 1)
    def unpack(pairs):
        for n, (i, j) in enumerate(PAIRS):
            if n not in pairs:
                continue
            r, l = row_id + i * TILE, lane_id + j * TILE
            value = gall[n * TILE : (n + 1) * TILE, :].astype(F32)
            value = jnp.where((r < rank) & (l < rank), value, 0.0)
            if i == j:
                value = value + jnp.where((r == l) & (r >= rank), 1.0, 0.0)
            amat[i * TILE : (i + 1) * TILE, j * TILE : (j + 1) * TILE] = value

    unpack(range(0, EARLY // TILE))
    wmat[...] = jnp.zeros_like(wmat)

    ticks = [0]

    def hook():
        ticks[0] += 1
        for job in jobs.pop(ticks[0], ()):
            job()

    for b in range(TILES):
        lo, hi = b * TILE, (b + 1) * TILE
        inv = tile_inverse(amat[lo:hi, lo:hi], hook)
        if b == 0:
            late.pass_on()
        if b:
            wmat[lo:hi, :lo] = dot(inv, wmat[lo:hi, :lo], precision=HIGHEST)
        wmat[lo:hi, lo:hi] = inv
        if b == 0:
            late.finish()
            unpack(range(EARLY // TILE, len(PAIRS)))
        if b < TILES - 1:
            strip = dot(inv, amat[lo:hi, hi:], precision=HIGHEST)
            amat[hi:, hi:] = amat[hi:, hi:] - dot(strip, strip, 0, 0, HIGHEST)
            wmat[hi:, :hi] = wmat[hi:, :hi] - dot(strip, wmat[lo:hi, :hi], 0, 0, HIGHEST)
    for tick in sorted(jobs):
        for job in jobs[tick]:
            job()

    w_hi, w_lo = split(wmat[...])
    pw = power[...]
    p_hi, p_lo = split(pw)
    ortho = dot(p_hi, w_hi, 1, 1) + dot(p_lo, w_hi, 1, 1) + dot(p_hi, w_lo, 1, 1)
    ortho_half = ortho.astype(BF16)
    outs = []
    mid = RANK // 2
    wide = 2 * SLAB
    chips = [y]
    for k in range(3):
        chips += [lax.rem(y + NY - 1 - k, NY), lax.rem(y + 1 + k, NY)]
    chips += [lax.rem(y + 4, NY)]
    columns = [pl.ds(pl.multiple_of(chip * wide, wide), wide) for chip in chips]

    def by_chip(n):
        chip, cols = chips[n], columns[n]
        t = jnp.concatenate([tall[2 * chip], tall[2 * chip + 1]], axis=1)
        upper = dot(w_hi[:mid, :mid], t[:mid]) + dot(w_lo[:mid, :mid], t[:mid])
        lower = dot(w_hi[mid:], t) + dot(w_lo[mid:], t)
        fac = jnp.concatenate([upper, lower], axis=0)
        if n == 0:
            own_fac[...] = jnp.where(c == 0, fac[:, :TILE], fac[:, TILE:])
        fh = fac.astype(BF16)
        fhalf[n] = fh
        back = dot(ortho_half, fh)
        nm[:, cols] = (full[:, cols] - (1.0 - MU_DECAY) * back).astype(BF16)
        copy = pltpu.make_async_copy(nm.at[:, cols], nm_hbm.at[:, cols], out_sem.at[n])
        copy.start()
        outs.append(copy)
        return fac[:, :TILE] * fac[:, :TILE] + fac[:, TILE:] * fac[:, TILE:]

    gather_t.own_across()
    squares = by_chip(0)
    for k in range(3):
        if k == 1:
            gather_t.step(3, 0)
            gather_t.step(3, 1)
        gather_t.far_across(k)
        squares = squares + by_chip(2 * k + 1)
        squares = squares + by_chip(2 * k + 2)
    gather_t.far_across(3)
    squares = squares + by_chip(7)
    col_sq = jnp.sum(squares, axis=1, keepdims=True)
    inv_col = lax.rsqrt(col_sq + EPS)
    inv_norm = jnp.broadcast_to(inv_col, (RANK, TILE)).T[:1, :]
    scaled = (ortho * (inv_norm * GAIN)).astype(BF16)
    for n in range(NY):
        cols = columns[n]
        up[:, cols] = dot(scaled, fhalf[n]).astype(BF16)
        copy = pltpu.make_async_copy(up.at[:, cols], up_hbm.at[:, cols], out_sem.at[NY + n])
        copy.start()
        outs.append(copy)
    nb_ref[...] = own_fac[...].T * inv_norm
    for copy in all_sent:
        copy.wait_send()
    for group in (gather_b, gather_t, early, late):
        group.drain()
    for copy in outs:
        copy.wait()


def local(momentum, gradient, basis, ranks, assignment):
    any_space = pl.BlockSpec(memory_space=pl.ANY)
    vmem = pl.BlockSpec(memory_space=pltpu.VMEM)
    dma = pltpu.SemaphoreType.DMA
    outs = pl.pallas_call(
        kernel,
        out_shape=(
            jax.ShapeDtypeStruct((MINE, FF), BF16),
            jax.ShapeDtypeStruct((MINE, FF), BF16),
            jax.ShapeDtypeStruct((SLAB, RANK), F32),
        ),
        in_specs=[any_space] * 5,
        out_specs=(any_space, any_space, vmem),
        scratch_shapes=[
            pltpu.VMEM((MINE, FF), BF16),
            pltpu.VMEM((MINE, FF), BF16),
            pltpu.VMEM((SLAB, RANK), F32),
            pltpu.SMEM((NX * NZ,), jnp.int32),
            pltpu.SMEM((NX * NZ,), jnp.int32),
            pltpu.VMEM((MINE, FF), F32),
            pltpu.VMEM((MINE, FF), BF16),
            pltpu.VMEM((16, SLAB, RANK), BF16),
            pltpu.VMEM((MINE, RANK), F32),
            pltpu.VMEM((PACKED, TILE), F32),
            pltpu.VMEM((EARLY // 2, TILE), BF16),
            pltpu.VMEM((EARLY // 2, TILE), BF16),
            pltpu.VMEM((2 * NY, EARLY // 16, TILE), BF16),
            pltpu.VMEM((LATE // 2, TILE), BF16),
            pltpu.VMEM((LATE // 2, TILE), BF16),
            pltpu.VMEM((2 * NY, LATE // 16, TILE), BF16),
            pltpu.VMEM((PACKED, TILE), BF16),
            pltpu.VMEM((2, NY, RANK, SLAB), F32),
            pltpu.VMEM((NY, RANK, SLAB), BF16),
            pltpu.VMEM((NY, RANK, SLAB), BF16),
            pltpu.VMEM((8, RANK, SLAB), BF16),
            pltpu.VMEM((8, RANK, SLAB), BF16),
            pltpu.VMEM((16, RANK, SLAB), BF16),
            pltpu.VMEM((RANK, RANK), F32),
            pltpu.VMEM((RANK, RANK), F32),
            pltpu.VMEM((NY, RANK, 2 * SLAB), BF16),
            pltpu.VMEM((RANK, SLAB), F32),
            pltpu.VMEM((MINE, FF), BF16),
            pltpu.VMEM((MINE, FF), BF16),
            pltpu.VMEM((4, 8, TILE), F32),
            pltpu.VMEM((18, 8, TILE), F32),
            dma((5,)),
            dma((16,)),
            dma((18,)),
            dma((18,)),
            dma((8 * PARTS,)),
            dma((8 * PARTS,)),
            dma((9 * PARTS,)),
            dma((9 * PARTS,)),
            dma((8 * PARTS,)),
            dma((8 * PARTS,)),
            dma((9 * PARTS,)),
            dma((9 * PARTS,)),
            dma((16,)),
            dma((16,)),
            dma((16,)),
            dma((16,)),
            dma((8 * PARTS,)),
            dma((8 * PARTS,)),
            dma((1,)),
            dma((1,)),
        ],
        compiler_params=pltpu.CompilerParams(
            collective_id=0, has_side_effects=True, vmem_limit_bytes=52 << 20
        ),
        cost_estimate=pl.CostEstimate(
            flops=4 << 30, bytes_accessed=5 << 20, transcendentals=0
        ),
    )(momentum[0], gradient[0], basis[0], ranks, assignment)
    return tuple(o[None] for o in outs)


def solution(mesh):
    torus = Mesh(mesh.devices.reshape(NX, NZ, NY, NC), (X, Z, Y, C))
    return jax.shard_map(
        local,
        mesh=torus,
        in_specs=(P(EXPERT, ROW, None), P(EXPERT, ROW, None), P(EXPERT, ROW, None), P(), P()),
        out_specs=(P(EXPERT, ROW, None), P(EXPERT, ROW, None), P(EXPERT, ROW, None)),
        check_vma=False,
    )
```
